32 devices in a mesh: fsdp: 4 (over y, x), ctx: 4 (over z), tp: 2 (over core).
Axes of the slice: x: 2, y: 2, z: 4, core: 2. Of those that a mesh axis runs over, the one named last changes fastest.
Arguments:
- tokens: bfloat16 [16, 1024, 1024], P('fsdp', 'ctx'), may hold values from -6 to 6
- segments: int32 [16, 1024], P('fsdp', 'ctx'), may hold values from 0 to 3, as said below
- gain_attn: bfloat16 [1024], P('fsdp'), may hold values from 0.099609375 to 1.8984375
- w_qkv: bfloat16 [3, 1024, 1024], P(None, 'fsdp', 'tp'), may hold values from -0.1875 to 0.1875
- w_out: bfloat16 [1024, 1024], P('tp', 'fsdp'), may hold values from -0.5 to 0.5
- gain_mlp: bfloat16 [1024], P('fsdp'), may hold values from 0.099609375 to 1.8984375
- w_up: bfloat16 [1024, 4096], P('fsdp', 'tp'), may hold values from -0.1875 to 0.1875
- w_down: bfloat16 [4096, 1024], P('tp', 'fsdp'), may hold values from -0.09375 to 0.09375
- cotangent: bfloat16 [16, 1024, 1024], P('fsdp', 'ctx'), may hold values from -6 to 6
Outputs:
- output: bfloat16 [16, 1024, 1024], P('fsdp', 'ctx')
- grad_tokens: bfloat16 [16, 1024, 1024], P('fsdp', 'ctx')
- grad_gain_attn: float32 [1024], P('fsdp')
- grad_w_qkv: float32 [3, 1024, 1024], P(None, 'fsdp', 'tp')
- grad_w_out: float32 [1024, 1024], P('tp', 'fsdp')
- grad_gain_mlp: float32 [1024], P('fsdp')
- grad_w_up: float32 [1024, 4096], P('fsdp', 'tp')
- grad_w_down: float32 [4096, 1024], P('tp', 'fsdp')
The draws below stay inside these ranges and needn't reach their ends.
Inputs may be any that keep to these rules, and one draw needn't show every extreme that they name: `segments`: within each row the numbers start at 0, never fall and rise by at most one from a position to the next; the largest is reached in some row of every draw. In each aligned block of 4 rows one row, drawn from the seed, keeps one document from position 128 to position 896.
All inputs are finite; a program needn't handle non-finite values.
Results may differ from the reference program's by a relative error of at most 0.019.
Values may be sent and summed in bfloat16 or wider, within the bound.
A program may use at most 192 MiB of HBM per device.

```python
from functools import partial
import jax
import jax.numpy as jnp
from jax import lax

D = 1024
HEADS = 16
HEAD_DIM = 64
FF = 4096
ROWS_DEV = 4
SEQ = 1024
DOC_GAP = 256
ROWS = 16
CTX_TOK = 256


def draw_segments(key, part):
    key = jax.random.fold_in(key, 7)
    first_key, second_key = jax.random.split(key)
    places = jnp.arange(SEQ)
    starts = (jax.random.randint(first_key, (ROWS, SEQ), 0, DOC_GAP) == 0).astype(jnp.int32)
    starts = jnp.where(places[None, :] == 0, 0, starts)
    chosen_row = jax.random.randint(second_key, (ROWS // ROWS_DEV,), 0, ROWS_DEV)
    chosen = jnp.arange(ROWS) % ROWS_DEV == jnp.repeat(chosen_row, ROWS_DEV)
    inner = (places > CTX_TOK // 2) & (places <= SEQ - CTX_TOK // 2)
    starts = jnp.where(chosen[:, None] & inner[None, :], 0, starts)
    first_block = jnp.arange(ROWS) < ROWS_DEV
    tail = places >= SEQ - 3
    starts = jnp.where((chosen & first_block)[:, None] & tail[None, :], 1, starts)
    return jnp.minimum(jnp.cumsum(starts, axis=1), 3).astype(jnp.int32)


def with_spikes(values, own_key, source, target, shards_of, factor):
    owner, partner = [(jnp.arange(values.shape[position]) // (values.shape[position] // shards_of)).reshape([-1 if axis == position else 1 for axis in range(values.ndim)]) for position in (source, target)]
    chosen = jax.random.permutation(own_key, shards_of)[partner]
    strong = (owner == chosen) | (owner == (partner + shards_of // 2) % shards_of)
    return jnp.where(strong, factor * values, values)


def steps_of(rng, shape, pieces, least, high):
    def one(dim, shards_of):
        heights = jax.random.uniform(jax.random.fold_in(jax.random.fold_in(rng, 6), dim), (shards_of,), jnp.float32, least / len(pieces), high / len(pieces))
        return jnp.repeat(jnp.exp(heights), shape[dim] // shards_of).reshape((-1,) + (1,) * (len(shape) - dim - 1))

    level = one(*pieces[0])
    for cut in pieces[1:]:
        level = level * one(*cut)
    return level


def centred(own_key, dims, deviation, bound, shards=(), kind=jnp.bfloat16):
    values = jax.random.normal(own_key, dims, jnp.float32) * deviation
    if len(shards) > 0:
        values = steps_of(own_key, dims, shards, -0.22, 0.18) * values
    return jnp.clip(values, min=-bound, max=bound).astype(kind)


def noise_with(own_key, dims, width, most, cuts, heavy, kind=jnp.bfloat16):
    values = width * jax.random.normal(own_key, dims, jnp.float32)
    if cuts:
        values = values * steps_of(own_key, dims, cuts, -0.22, 0.18)
    return jnp.clip(with_spikes(values, jax.random.fold_in(own_key, 3), *heavy), -most, most).astype(kind)


def setup_inputs(seed: int = 0) -> dict:
    seeds = jax.random.split(jax.random.key(seed), 10)
    tokens = centred(seeds[0], (ROWS, SEQ, D), 1.0, 6.0, ((0, 4), (1, 4)))
    segments = draw_segments(jax.random.fold_in(seeds[9], 71), 0)
    gain_attn = jnp.clip(1.0 + 0.18 * jax.random.normal(seeds[2], (D,), jnp.float32), 0.099609375, 1.8984375).astype(jnp.bfloat16)
    w_qkv = centred(seeds[3], (3, D, D), D ** -0.5, 0.1875, ((1, 4), (2, 2)))
    w_out = centred(seeds[4], (D, D), (D // 8) ** -0.5, 0.5, ((0, 2), (1, 4)))
    gain_mlp = jnp.clip(1.0 + 0.18 * jax.random.normal(seeds[5], (D,), jnp.float32), 0.099609375, 1.8984375).astype(jnp.bfloat16)
    w_up = centred(seeds[6], (D, FF), D ** -0.5, 0.1875, ((0, 4), (1, 2)))
    w_down = centred(seeds[7], (FF, D), FF ** -0.5, 0.09375, ((0, 2), (1, 4)))
    cotangent = noise_with(seeds[8], (ROWS, SEQ, D), 1.0, 6.0, ((0, 4), (1, 4)), (0, 2, 4, 2.0))
    return dict(tokens=tokens, segments=segments, gain_attn=gain_attn, w_qkv=w_qkv, w_out=w_out, gain_mlp=gain_mlp, w_up=w_up, w_down=w_down, cotangent=cotangent)


@jax.custom_vjp
def low(v):
    return lax.optimization_barrier(v.astype(jnp.bfloat16)).astype(jnp.float32)

@jax.custom_vjp
def low_back(v):
    return v

def low_keep(v):
    return (low(v), None)

def low_pass(kept, grad):
    return (grad,)

def back_keep(v):
    return (v, None)

def back_low(kept, grad):
    return (low(grad),)
low.defvjp(low_keep, low_pass)
low_back.defvjp(back_keep, back_low)
EPSILON = 1e-05
HIGHEST = lax.Precision.HIGHEST

def layer_norm(values, gain_vec):
    row_mean = lax.optimization_barrier(jnp.mean(values, axis=-1, keepdims=True))
    centered = values - row_mean
    inverse = lax.rsqrt(lax.optimization_barrier(jnp.mean(centered * centered, axis=-1, keepdims=True)) + EPSILON)
    return centered * inverse * gain_vec

def attend_row(packed):
    queries, key_rows, value_rows, segment = packed
    raw_scores = low_back(jnp.einsum('qhd,khd->hqk', queries, key_rows, precision=HIGHEST))
    scores = raw_scores * HEAD_DIM ** (-0.5)
    places = jnp.arange(SEQ)
    allowed = (segment[:, None] == segment[None, :]) & (places[:, None] >= places[None, :])
    scores = jnp.where(allowed[None], scores, -1e+30)
    row_top = lax.optimization_barrier(jnp.max(scores, axis=-1, keepdims=True))
    weights = jnp.exp(scores - row_top)
    row_probs = low(weights / lax.optimization_barrier(jnp.sum(weights, axis=-1, keepdims=True)))
    return jnp.einsum('hqk,khd->qhd', row_probs, value_rows, precision=HIGHEST)

def forward(segments, inputs, gain_attn, w_qkv, w_out, gain_mlp, w_up, w_down):
    first = low(layer_norm(inputs, gain_attn))
    projected = jnp.einsum('rsd,tde->rtse', first, w_qkv, precision=HIGHEST)
    projected = low_back(low(projected)).reshape(ROWS, 3, SEQ, HEADS, HEAD_DIM)
    mixed = lax.map(jax.checkpoint(attend_row), (projected[:, 0], projected[:, 1], projected[:, 2], segments))
    mixed = low_back(low(mixed)).reshape(ROWS, SEQ, D)
    branch = low_back(jnp.einsum('rse,ed->rsd', mixed, w_out, precision=HIGHEST))
    resid = inputs + branch
    second = low(layer_norm(resid, gain_mlp))
    up_proj = low_back(jnp.einsum('rsd,df->rsf', second, w_up, precision=HIGHEST))
    hidden = low(jax.nn.gelu(up_proj, approximate=True))
    mlp_output = low_back(jnp.einsum('rsf,fd->rsd', hidden, w_down, precision=HIGHEST))
    return resid + mlp_output

def reference(tokens, segments, gain_attn, w_qkv, w_out, gain_mlp, w_up, w_down, cotangent):
    floats = tuple((array.astype(jnp.float32) for array in (tokens, gain_attn, w_qkv, w_out, gain_mlp, w_up, w_down)))
    result, pullback = jax.vjp(partial(forward, segments), *floats)
    grads = pullback(cotangent.astype(jnp.float32))
    return (result.astype(jnp.bfloat16), grads[0].astype(jnp.bfloat16), grads[1], grads[2], grads[3], grads[4], grads[5], grads[6])
```

```python
from functools import partial

import jax
import jax.numpy as jnp
from jax import lax
from jax.experimental import pallas as pl
from jax.experimental.pallas import tpu as pltpu
from jax.sharding import PartitionSpec as P

HEAD_DIM = 64
EPSILON = 1e-05
BF16 = jnp.bfloat16
F32 = jnp.float32


def layer_norm(values, gain_vec):
    row_mean = jnp.mean(values, axis=-1, keepdims=True)
    centered = values - row_mean
    inverse = lax.rsqrt(jnp.mean(centered * centered, axis=-1, keepdims=True) + EPSILON)
    return centered * inverse * gain_vec


def dot(a, b, over=(1, 0)):
    return lax.dot_general(a, b, (((over[0],), (over[1],)), ((), ())), preferred_element_type=F32)


def query_block(length):
    return 256 if length % 256 == 0 else length


def fill_bias(bias, seg_row, seg_col):
    length = bias.shape[0]
    block = query_block(length)
    for start in range(0, length, block):
        stop = start + block
        keys = lax.broadcasted_iota(jnp.int32, (stop, block), 0)
        queries = lax.broadcasted_iota(jnp.int32, (stop, block), 1) + start
        same = seg_col[:stop, :] == seg_row[:, start:stop]
        bias[:stop, start:stop] = jnp.where(same & (keys <= queries), 0.0, -1e30)


def attend_kernel(seg_row, seg_col, q_ref, k_ref, v_ref, o_ref, bias):
    @pl.when(pl.program_id(0) == 0)
    def _():
        fill_bias(bias, seg_row, seg_col)

    length, width = q_ref.shape
    block = query_block(length)
    for start in range(0, length, block):
        stop = start + block
        parts = []
        for low in range(0, width, HEAD_DIM):
            lanes = slice(low, low + HEAD_DIM)
            queries = q_ref[start:stop, lanes] * HEAD_DIM**-0.5
            scores = dot(k_ref[:stop, lanes], queries, (1, 1)) + bias[:stop, start:stop]
            weights = jnp.exp(scores - jnp.max(scores, axis=0, keepdims=True))
            total = jnp.sum(weights, axis=0, keepdims=True)
            mixed = dot(v_ref[:stop, lanes], weights.astype(BF16), (0, 0))
            parts.append(mixed / total)
        o_ref[start:stop, :] = jnp.concatenate(parts, axis=0).T.astype(BF16)


def attend_back_kernel(seg_row, seg_col, q_ref, k_ref, v_ref, do_ref, dq_ref, dk_ref, dv_ref, bias, dk_sum, dv_sum):
    @pl.when(pl.program_id(0) == 0)
    def _():
        fill_bias(bias, seg_row, seg_col)

    length, width = q_ref.shape
    block = query_block(length)
    dk_sum[...] = jnp.zeros_like(dk_sum)
    dv_sum[...] = jnp.zeros_like(dv_sum)
    for start in range(0, length, block):
        stop = start + block
        parts = []
        for head, low in enumerate(range(0, width, HEAD_DIM)):
            lanes = slice(low, low + HEAD_DIM)
            queries = q_ref[start:stop, lanes] * HEAD_DIM**-0.5
            keys = k_ref[:stop, lanes]
            grad = do_ref[start:stop, lanes]
            scores = dot(keys, queries, (1, 1)) + bias[:stop, start:stop]
            weights = jnp.exp(scores - jnp.max(scores, axis=0, keepdims=True))
            probs = weights * (1.0 / jnp.sum(weights, axis=0, keepdims=True))
            grad_probs = dot(v_ref[:stop, lanes], grad, (1, 1))
            inner = jnp.sum(probs * grad_probs, axis=0, keepdims=True)
            grad_scores = (probs * (grad_probs - inner)).astype(BF16)
            dv_sum[head, :stop, :] += dot(probs.astype(BF16), grad)
            dk_sum[head, :stop, :] += dot(grad_scores, queries)
            parts.append(dot(keys, grad_scores, (0, 0)) * HEAD_DIM**-0.5)
        dq_ref[start:stop, :] = jnp.concatenate(parts, axis=0).T.astype(BF16)
    for head, low in enumerate(range(0, width, HEAD_DIM)):
        dk_ref[:, low : low + HEAD_DIM] = dk_sum[head].astype(BF16)
        dv_ref[:, low : low + HEAD_DIM] = dv_sum[head].astype(BF16)


def attention_call(kernel, outputs, scratch, segment, *arrays):
    length, columns = arrays[0].shape
    width = 2 * HEAD_DIM if columns % (2 * HEAD_DIM) == 0 else columns
    pair = pl.BlockSpec((length, width), lambda h: (0, h))
    flops = 4 * length * length * columns * (1 if outputs == 1 else 3)
    shape = jax.ShapeDtypeStruct((length, columns), BF16)
    return pl.pallas_call(
        kernel,
        grid=(columns // width,),
        in_specs=[
            pl.BlockSpec((1, length), lambda h: (0, 0)),
            pl.BlockSpec((length, 1), lambda h: (0, 0)),
        ]
        + [pair] * len(arrays),
        out_specs=[pair] * outputs,
        out_shape=[shape] * outputs,
        scratch_shapes=[pltpu.VMEM((length, length), F32)]
        + [pltpu.VMEM((width // HEAD_DIM, length, HEAD_DIM), F32)] * scratch,
        compiler_params=pltpu.CompilerParams(vmem_limit_bytes=40 * 1024 * 1024),
        cost_estimate=pl.CostEstimate(
            flops=flops,
            bytes_accessed=2 * length * columns * (len(arrays) + outputs),
            transcendentals=length * length * columns // HEAD_DIM,
        ),
    )(segment.reshape(1, length), segment.reshape(length, 1), *arrays)


def swap(value, axis, size, step):
    return lax.ppermute(value, axis, [(i, i ^ step) for i in range(size)])


def take(value, index, dim):
    return lax.dynamic_index_in_dim(value, index, dim, keepdims=False)


def after(value, *others):
    return lax.optimization_barrier((value,) + others)[0]


def pieces(value, axis, size):
    return [value] + [swap(value, axis, size, step) for step in range(1, size)]


def assemble(parts, axis, dim):
    me = lax.axis_index(axis)
    each = parts[0].shape[dim]
    shape = list(parts[0].shape)
    shape[dim] = each * len(parts)
    whole = jnp.zeros(shape, parts[0].dtype)
    for step, part in enumerate(parts):
        whole = lax.dynamic_update_slice_in_dim(whole, part, (me ^ step) * each, dim)
    return whole


def to_rows(value, axis, size):
    me = lax.axis_index(axis)
    parts = [take(value, me, 0)[None]]
    for step in range(1, size):
        parts.append(swap(take(value, me ^ step, 0)[None], axis, size, step))
    return assemble(parts, axis, 0)


def butterfly(value, axis, size):
    step = 1
    while step < size:
        value = value + swap(value, axis, size, step)
        step *= 2
    return value


def shards(sizes, tokens, segments, gain_attn, w_qkv, w_out, gain_mlp, w_up, w_down, cotangent):
    n_fsdp, n_ctx, n_tp = sizes["fsdp"], sizes["ctx"], sizes["tp"]
    row_count, local_len, width = tokens.shape
    group = row_count // n_ctx
    share = local_len // n_tp
    fsdp, tp, ctx = lax.axis_index("fsdp"), lax.axis_index("tp"), lax.axis_index("ctx")
    count = group * n_ctx * local_len
    length = n_ctx * local_len

    def row_in(array):
        cut = take(array.reshape(n_ctx, group, n_tp, share, width), tp, 2)
        got = to_rows(cut, "ctx", n_ctx)
        full = assemble(pieces(got[:, :, None], "tp", n_tp), "tp", 2)
        return full.transpose(1, 0, 2, 3, 4).reshape(count, width)

    def my_share(array):
        cut = array.reshape(group, n_ctx, n_tp, share, array.shape[-1])
        return take(cut, tp, 2).transpose(1, 0, 2, 3)

    def share_sum(partial_sum):
        cut = partial_sum.reshape(group, n_ctx, n_tp, share, width)
        total = take(cut, tp, 2).astype(F32)
        for step in range(1, n_tp):
            total = total + swap(take(cut, tp ^ step, 2), "tp", n_tp, step).astype(F32)
        return total.transpose(1, 0, 2, 3)

    def row_out(shared):
        got = to_rows(shared, "ctx", n_ctx)
        full = assemble(pieces(got[:, :, None], "tp", n_tp), "tp", 2)
        return full.reshape(row_count, local_len, width)

    def tp_sum(partial_sum):
        low = partial_sum.astype(BF16)
        if n_tp == 2:
            return low.astype(F32) + swap(low, "tp", n_tp, 1).astype(F32)
        return lax.psum(low.astype(F32), "tp")

    gains = assemble(pieces(jnp.stack([gain_attn, gain_mlp]), "fsdp", n_fsdp), "fsdp", 1)
    gain_one, gain_two = gains[0].astype(F32), gains[1].astype(F32)
    tokens_row = row_in(tokens)
    own_segments = to_rows(segments.reshape(n_ctx, group, local_len), "ctx", n_ctx)
    own_segments = own_segments.transpose(1, 0, 2).reshape(group, length)

    qkv_parts = pieces(w_qkv, "fsdp", n_fsdp)
    out_parts = pieces(after(w_out, tokens_row), "fsdp", n_fsdp)
    up_parts = pieces(after(w_up, qkv_parts[-1]), "fsdp", n_fsdp)
    grad_output = row_in(after(cotangent, tokens_row))
    down_parts = pieces(after(w_down, out_parts[-1], up_parts[1]), "fsdp", n_fsdp)

    flat_tokens = tokens_row.astype(F32)
    low_one = layer_norm(flat_tokens, gain_one).astype(BF16)
    qkv_weight = assemble(qkv_parts, "fsdp", 1)
    queries, keys, values = (dot(low_one, qkv_weight[t]).astype(BF16) for t in range(3))

    def by_row(kernel, outputs, scratch, *arrays):
        rows = []
        for row in range(group):
            cut = [a[row * length : (row + 1) * length] for a in arrays]
            rows.append(attention_call(kernel, outputs, scratch, own_segments[row], *cut))
        return [jnp.concatenate(parts, axis=0) if group > 1 else parts[0] for parts in zip(*rows)]

    (mixed,) = by_row(attend_kernel, 1, 0, queries, keys, values)
    out_weight = assemble(out_parts, "fsdp", 1)
    resid = flat_tokens + tp_sum(dot(mixed, out_weight))
    low_two = layer_norm(resid, gain_two).astype(BF16)
    up_weight = assemble(up_parts, "fsdp", 0)
    up_proj = dot(low_two, up_weight)
    hidden, gelu_back = jax.vjp(partial(jax.nn.gelu, approximate=True), up_proj)
    hidden = hidden.astype(BF16)
    down_weight = assemble(down_parts, "fsdp", 1)
    grad_hidden = dot(grad_output, down_weight, (1, 1))
    grad_up_act = gelu_back(grad_hidden)[0].astype(BF16)
    grad_norm_two = tp_sum(dot(grad_up_act, up_weight, (1, 1)))

    def reduce_rows(make):
        total = make(fsdp)
        for step in range(1, n_fsdp):
            total = total + swap(make(fsdp ^ step).astype(BF16), "fsdp", n_fsdp, step).astype(F32)
        block = total.shape
        cut = total.astype(BF16).reshape((n_ctx, block[0] // n_ctx) + block[1:])
        part = take(cut, ctx, 0).astype(F32)
        for step in range(1, n_ctx):
            part = part + swap(take(cut, ctx ^ step, 0), "ctx", n_ctx, step).astype(F32)
        return assemble(pieces(part.astype(BF16), "ctx", n_ctx), "ctx", 0).astype(F32)

    def columns(array, index):
        each = array.shape[1] // n_fsdp
        return lax.dynamic_slice_in_dim(array, index * each, each, 1)

    grad_down = reduce_rows(lambda j: dot(hidden, columns(grad_output, j), (0, 0)))
    grad_up = reduce_rows(lambda j: dot(columns(low_two, j), grad_up_act, (0, 0)))

    mlp_part = dot(hidden, down_weight).astype(BF16)
    result = row_out((my_share(resid) + share_sum(mlp_part)).astype(BF16))

    _, norm_back_two = jax.vjp(layer_norm, resid, gain_two)
    grad_through, grad_gain_two = norm_back_two(grad_norm_two)
    grad_resid = grad_output.astype(F32) + grad_through
    grad_branch = grad_resid.astype(BF16)
    grad_mixed = dot(grad_branch, out_weight, (1, 1)).astype(BF16)
    grad_out_weight = reduce_rows(lambda j: dot(mixed, columns(grad_branch, j), (0, 0)))

    grads = by_row(attend_back_kernel, 3, 2, queries, keys, values, grad_mixed)
    grad_packed = jnp.concatenate(grads, axis=1)
    grad_norm_one = sum(dot(grads[t], qkv_weight[t], (1, 1)) for t in range(3)).astype(BF16)
    grad_norm_one = share_sum(grad_norm_one)
    grad_qkv = reduce_rows(lambda j: dot(columns(low_one, j), grad_packed, (0, 0)))
    grad_qkv = grad_qkv.reshape(width // n_fsdp, 3, -1).transpose(1, 0, 2)

    _, norm_back_one = jax.vjp(layer_norm, my_share(flat_tokens), gain_one)
    grad_flat, grad_gain_one = norm_back_one(grad_norm_one)
    grad_tokens = row_out((my_share(grad_resid) + grad_flat).astype(BF16))
    grad_gain_one = butterfly(grad_gain_one, "tp", n_tp)
    gain_grads = jnp.stack([grad_gain_one, grad_gain_two])
    gain_grads = butterfly(butterfly(gain_grads, "fsdp", n_fsdp), "ctx", n_ctx)
    gain_grads = columns(gain_grads, fsdp)
    return (result, grad_tokens, gain_grads[0], grad_qkv, grad_out_weight, gain_grads[1], grad_up, grad_down)


def solution(mesh):
    return jax.shard_map(
        partial(shards, dict(mesh.shape)),
        mesh=mesh,
        in_specs=(
            P("fsdp", "ctx", None),
            P("fsdp", "ctx"),
            P("fsdp"),
            P(None, "fsdp", "tp"),
            P("tp", "fsdp"),
            P("fsdp"),
            P("fsdp", "tp"),
            P("tp", "fsdp"),
            P("fsdp", "ctx", None),
        ),
        out_specs=(
            P("fsdp", "ctx", None),
            P("fsdp", "ctx", None),
            P("fsdp"),
            P(None, "fsdp", "tp"),
            P("tp", "fsdp"),
            P("fsdp"),
            P("fsdp", "tp"),
            P("tp", "fsdp"),
        ),
        check_vma=False,
    )
```

```python
from functools import partial

import jax
import jax.numpy as jnp
from jax import lax
from jax.experimental import pallas as pl
from jax.experimental.pallas import tpu as pltpu
from jax.sharding import PartitionSpec as P

HEAD_DIM = 64
EPSILON = 1e-05
BF16 = jnp.bfloat16
F32 = jnp.float32


def layer_norm(values, gain_vec):
    row_mean = jnp.mean(values, axis=-1, keepdims=True)
    centered = values - row_mean
    inverse = lax.rsqrt(jnp.mean(centered * centered, axis=-1, keepdims=True) + EPSILON)
    return centered * inverse * gain_vec


def dot(a, b, over=(1, 0)):
    return lax.dot_general(a, b, (((over[0],), (over[1],)), ((), ())), preferred_element_type=F32)


def query_block(length):
    return 256 if length % 256 == 0 else length


def fill_bias(bias, seg_row, seg_col):
    length = bias.shape[0]
    block = query_block(length)
    for start in range(0, length, block):
        stop = start + block
        keys = lax.broadcasted_iota(jnp.int32, (stop, block), 0)
        queries = lax.broadcasted_iota(jnp.int32, (stop, block), 1) + start
        same = seg_col[:stop, :] == seg_row[:, start:stop]
        bias[:stop, start:stop] = jnp.where(same & (keys <= queries), 0.0, -1e30)


def attend_kernel(seg_row, seg_col, q_ref, k_ref, v_ref, o_ref, bias):
    @pl.when(pl.program_id(0) == 0)
    def _():
        fill_bias(bias, seg_row, seg_col)

    length, width = q_ref.shape
    block = query_block(length)
    for start in range(0, length, block):
        stop = start + block
        parts = []
        for low in range(0, width, HEAD_DIM):
            lanes = slice(low, low + HEAD_DIM)
            queries = q_ref[start:stop, lanes] * HEAD_DIM**-0.5
            scores = dot(k_ref[:stop, lanes], queries, (1, 1)) + bias[:stop, start:stop]
            weights = jnp.exp(scores - jnp.max(scores, axis=0, keepdims=True))
            total = jnp.sum(weights, axis=0, keepdims=True)
            mixed = dot(v_ref[:stop, lanes], weights.astype(BF16), (0, 0))
            parts.append(mixed / total)
        o_ref[start:stop, :] = jnp.concatenate(parts, axis=0).T.astype(BF16)


def attend_back_kernel(seg_row, seg_col, q_ref, k_ref, v_ref, do_ref, dq_ref, dk_ref, dv_ref, bias, dk_sum, dv_sum):
    @pl.when(pl.program_id(0) == 0)
    def _():
        fill_bias(bias, seg_row, seg_col)

    length, width = q_ref.shape
    block = query_block(length)
    dk_sum[...] = jnp.zeros_like(dk_sum)
    dv_sum[...] = jnp.zeros_like(dv_sum)
    for start in range(0, length, block):
        stop = start + block
        parts = []
        for head, low in enumerate(range(0, width, HEAD_DIM)):
            lanes = slice(low, low + HEAD_DIM)
            queries = q_ref[start:stop, lanes] * HEAD_DIM**-0.5
            keys = k_ref[:stop, lanes]
            grad = do_ref[start:stop, lanes]
            scores = dot(keys, queries, (1, 1)) + bias[:stop, start:stop]
            weights = jnp.exp(scores - jnp.max(scores, axis=0, keepdims=True))
            probs = weights * (1.0 / jnp.sum(weights, axis=0, keepdims=True))
            grad_probs = dot(v_ref[:stop, lanes], grad, (1, 1))
            inner = jnp.sum(probs * grad_probs, axis=0, keepdims=True)
            grad_scores = (probs * (grad_probs - inner)).astype(BF16)
            dv_sum[head, :stop, :] += dot(probs.astype(BF16), grad)
            dk_sum[head, :stop, :] += dot(grad_scores, queries)
            parts.append(dot(keys, grad_scores, (0, 0)) * HEAD_DIM**-0.5)
        dq_ref[start:stop, :] = jnp.concatenate(parts, axis=0).T.astype(BF16)
    for head, low in enumerate(range(0, width, HEAD_DIM)):
        dk_ref[:, low : low + HEAD_DIM] = dk_sum[head].astype(BF16)
        dv_ref[:, low : low + HEAD_DIM] = dv_sum[head].astype(BF16)


def attention_call(kernel, outputs, scratch, segment, *arrays):
    length, columns = arrays[0].shape
    width = 2 * HEAD_DIM if columns % (2 * HEAD_DIM) == 0 else columns
    pair = pl.BlockSpec((length, width), lambda h: (0, h))
    flops = 4 * length * length * columns * (1 if outputs == 1 else 3)
    shape = jax.ShapeDtypeStruct((length, columns), BF16)
    return pl.pallas_call(
        kernel,
        grid=(columns // width,),
        in_specs=[
            pl.BlockSpec((1, length), lambda h: (0, 0)),
            pl.BlockSpec((length, 1), lambda h: (0, 0)),
        ]
        + [pair] * len(arrays),
        out_specs=[pair] * outputs,
        out_shape=[shape] * outputs,
        scratch_shapes=[pltpu.VMEM((length, length), F32)]
        + [pltpu.VMEM((width // HEAD_DIM, length, HEAD_DIM), F32)] * scratch,
        compiler_params=pltpu.CompilerParams(vmem_limit_bytes=40 * 1024 * 1024),
        cost_estimate=pl.CostEstimate(
            flops=flops,
            bytes_accessed=2 * length * columns * (len(arrays) + outputs),
            transcendentals=length * length * columns // HEAD_DIM,
        ),
    )(segment.reshape(1, length), segment.reshape(length, 1), *arrays)


def swap(value, axis, size, step):
    return lax.ppermute(value, axis, [(i, i ^ step) for i in range(size)])


def take(value, index, dim):
    return lax.dynamic_index_in_dim(value, index, dim, keepdims=False)


def mark(value):
    return value[(0,) * value.ndim].astype(F32) * 0.0


def after(value, *others):
    for other in others:
        value = value + mark(other).astype(value.dtype)
    return value


def pieces(value, axis, size):
    return [value] + [swap(value, axis, size, step) for step in range(1, size)]


def half_of(rows):
    return rows // 2 // 16 * 16 if rows >= 32 else rows // 2


def gather(value, size):
    if size != 4:
        return pieces(value, "fsdp", size)
    half = half_of(value.shape[0])
    near, other = swap(value, "fsdp", size, 1), swap(value, "fsdp", size, 2)
    upper = swap(near[:half], "fsdp", size, 2)
    lower = swap(other[half:], "fsdp", size, 1)
    return [value, near, other, jnp.concatenate([upper, lower], axis=0)]


def reduce_blocks(make, size, hold=None):
    me = lax.axis_index("fsdp")
    if size != 4:
        terms = [make(me ^ step).astype(BF16) for step in range(1, size)]
        total = make(me)
        for step, term in enumerate(terms):
            total = total + swap(term, "fsdp", size, step + 1).astype(F32)
        return total, terms
    far = make(me ^ 3).astype(BF16)
    rows = far.shape[0]
    half = half_of(rows)
    upper = swap(far[:half], "fsdp", size, 1).astype(F32)
    lower = swap(far[half:], "fsdp", size, 2).astype(F32)
    if hold is not None:
        upper, lower = upper + hold, lower + hold
    other = (make(me ^ 2) + jnp.pad(upper, ((0, rows - half), (0, 0)))).astype(BF16)
    near = (make(me ^ 1) + jnp.pad(lower, ((half, 0), (0, 0)))).astype(BF16)
    near, other = lax.optimization_barrier((near, other))
    total = make(me) + swap(near, "fsdp", size, 1).astype(F32) + swap(other, "fsdp", size, 2).astype(F32)
    return total, [near, other]


def assemble(parts, axis, dim):
    me = lax.axis_index(axis)
    each = parts[0].shape[dim]
    shape = list(parts[0].shape)
    shape[dim] = each * len(parts)
    whole = jnp.zeros(shape, parts[0].dtype)
    for step, part in enumerate(parts):
        whole = lax.dynamic_update_slice_in_dim(whole, part, (me ^ step) * each, dim)
    return whole


def to_parts(value, axis, size):
    me = lax.axis_index(axis)
    parts = [take(value, me, 0)[None]]
    for step in range(1, size):
        parts.append(swap(take(value, me ^ step, 0)[None], axis, size, step))
    return parts


def to_rows(value, axis, size):
    return assemble(to_parts(value, axis, size), axis, 0)


def butterfly(value, axis, size):
    step = 1
    while step < size:
        value = value + swap(value, axis, size, step)
        step *= 2
    return value


def shards(sizes, tokens, segments, gain_attn, w_qkv, w_out, gain_mlp, w_up, w_down, cotangent):
    n_fsdp, n_ctx, n_tp = sizes["fsdp"], sizes["ctx"], sizes["tp"]
    row_count, local_len, width = tokens.shape
    group = row_count // n_ctx
    share = local_len // n_tp
    fsdp, tp, ctx = lax.axis_index("fsdp"), lax.axis_index("tp"), lax.axis_index("ctx")
    count = group * n_ctx * local_len
    length = n_ctx * local_len

    def spread(got):
        full = assemble(pieces(got[:, :, None], "tp", n_tp), "tp", 2)
        return full.transpose(1, 0, 2, 3, 4).reshape(count, width)

    def row_in(array):
        cut = take(array.reshape(n_ctx, group, n_tp, share, width), tp, 2)
        return spread(lax.all_to_all(cut, "ctx", split_axis=0, concat_axis=0, tiled=True))

    def my_share(array):
        cut = array.reshape(group, n_ctx, n_tp, share, array.shape[-1])
        return take(cut, tp, 2).transpose(1, 0, 2, 3)

    def share_sum(partial_sum):
        cut = partial_sum.reshape(group, n_ctx, n_tp, share, width)
        total = take(cut, tp, 2).astype(F32)
        for step in range(1, n_tp):
            total = total + swap(take(cut, tp ^ step, 2), "tp", n_tp, step).astype(F32)
        return total.transpose(1, 0, 2, 3)

    def rows_of(got):
        full = assemble(pieces(got[:, :, None], "tp", n_tp), "tp", 2)
        return full.reshape(row_count, local_len, width)

    def tp_sum(partial_sum):
        low = partial_sum.astype(BF16)
        if n_tp == 2:
            return low.astype(F32) + swap(low, "tp", n_tp, 1).astype(F32)
        return lax.psum(low.astype(F32), "tp")

    each, heads_width = w_qkv.shape[1], w_qkv.shape[2]
    gain_rows = -(-2 * each // heads_width)
    gain_pad = gain_rows * heads_width - 2 * each
    packed_gains = jnp.pad(jnp.concatenate([gain_attn, gain_mlp]), (0, gain_pad)).reshape(gain_rows, heads_width)
    qkv_gains = jnp.concatenate([w_qkv.reshape(3 * each, heads_width), packed_gains], axis=0)
    cut = take(tokens.reshape(n_ctx, group, n_tp, share, width), tp, 2)
    numbers = segments.reshape(n_ctx, group, 1, local_len).astype(BF16)
    numbers = jnp.pad(numbers, ((0, 0), (0, 0), (0, 15), (0, width - local_len)))
    got = to_parts(jnp.concatenate([cut, numbers], axis=2), "ctx", n_ctx)
    tokens_row = spread(assemble([part[:, :, :share] for part in got], "ctx", 0))
    own_segments = assemble([part[:, :, share, :local_len] for part in got], "ctx", 0).transpose(1, 0, 2).reshape(group, length).astype(jnp.int32)

    qkv_parts = gather(qkv_gains, n_fsdp)
    out_parts = gather(after(w_out, qkv_parts[1]), n_fsdp)
    up_parts = gather(after(w_up, qkv_parts[1]), n_fsdp)
    grad_output = row_in(after(cotangent, tokens_row))
    down_parts = gather(after(w_down, qkv_parts[1]), n_fsdp)
    all_gains = [part[3 * each :].reshape(-1)[: 2 * each].reshape(2, each) for part in qkv_parts]
    gains = assemble(all_gains, "fsdp", 1)
    gain_one, gain_two = gains[0].astype(F32), gains[1].astype(F32)
    qkv_parts = [part[: 3 * each].reshape(3, each, heads_width) for part in qkv_parts]

    flat_tokens = tokens_row.astype(F32)
    low_one = layer_norm(flat_tokens, gain_one).astype(BF16)
    qkv_weight = assemble(qkv_parts, "fsdp", 1)
    queries, keys, values = (dot(low_one, qkv_weight[t]).astype(BF16) for t in range(3))

    def by_row(kernel, outputs, scratch, *arrays):
        rows = []
        for row in range(group):
            cut = [a[row * length : (row + 1) * length] for a in arrays]
            rows.append(attention_call(kernel, outputs, scratch, own_segments[row], *cut))
        return [jnp.concatenate(parts, axis=0) if group > 1 else parts[0] for parts in zip(*rows)]

    (mixed,) = by_row(attend_kernel, 1, 0, queries, keys, values)
    out_weight = assemble(out_parts, "fsdp", 1)
    resid = flat_tokens + tp_sum(dot(mixed, out_weight))
    low_two = layer_norm(resid, gain_two).astype(BF16)
    up_weight = assemble(up_parts, "fsdp", 0)
    up_proj = dot(low_two, up_weight)
    hidden, gelu_back = jax.vjp(partial(jax.nn.gelu, approximate=True), up_proj)
    hidden = hidden.astype(BF16)
    down_weight = assemble(down_parts, "fsdp", 1)
    grad_hidden = dot(grad_output, down_weight, (1, 1))
    grad_up_act = gelu_back(grad_hidden)[0].astype(BF16)
    norm_two_part = dot(grad_up_act, up_weight, (1, 1)).astype(BF16)
    grad_norm_two = tp_sum(norm_two_part)

    def columns(array, index):
        each = array.shape[1] // n_fsdp
        return lax.dynamic_slice_in_dim(array, index * each, each, 1)

    _, norm_back_two = jax.vjp(layer_norm, resid, gain_two)
    grad_through, grad_gain_two = norm_back_two(grad_norm_two)
    grad_resid = grad_output.astype(F32) + grad_through
    grad_branch = grad_resid.astype(BF16)
    grad_mixed = dot(grad_branch, out_weight, (1, 1)).astype(BF16)
    hold = mark(grad_branch)
    down_total, _ = reduce_blocks(lambda j: dot(hidden, columns(grad_output, j), (0, 0)), n_fsdp)
    down_total = lax.optimization_barrier(down_total.astype(BF16))
    grad_down = lax.psum(down_total, "ctx")
    up_total, up_sent = reduce_blocks(lambda j: dot(columns(low_two, j), grad_up_act, (0, 0)), n_fsdp, hold)
    mlp_part = dot(hidden, down_weight).astype(BF16)
    shared = (my_share(resid) + share_sum(mlp_part) + hold).astype(BF16)
    grad_mixed = after(grad_mixed, down_total, *up_sent)
    result = rows_of(lax.all_to_all(shared, "ctx", split_axis=0, concat_axis=0, tiled=True))

    grads = by_row(attend_back_kernel, 3, 2, queries, keys, values, grad_mixed)
    norm_one_part = sum(dot(grads[t], qkv_weight[t], (1, 1)) for t in range(3)).astype(BF16)
    grad_norm_one = share_sum(norm_one_part)
    done = mark(grads[0])
    grad_packed = jnp.concatenate(grads, axis=1)
    grad_up = lax.psum((up_total + done + mark(grad_down)).astype(BF16), "ctx")
    out_total, _ = reduce_blocks(lambda j: dot(mixed, columns(grad_branch, j), (0, 0)), n_fsdp, done)
    qkv_total, _ = reduce_blocks(lambda j: dot(columns(low_one, j), grad_packed, (0, 0)), n_fsdp)
    qkv_total = qkv_total.reshape(each, 3, heads_width).transpose(1, 0, 2)
    _, norm_back_one = jax.vjp(layer_norm, my_share(flat_tokens), gain_one)
    grad_flat, grad_gain_one = norm_back_one(grad_norm_one)
    tokens_got = to_rows((my_share(grad_resid) + grad_flat).astype(BF16), "ctx", n_ctx)
    grad_tokens = rows_of(tokens_got)
    first = mark(grad_up) + mark(tokens_got)
    grad_out_weight, grad_qkv = lax.psum(((out_total + first).astype(BF16), (qkv_total + first).astype(BF16)), "ctx")
    grad_down, grad_up, grad_out_weight, grad_qkv = (
        array.astype(F32) for array in (grad_down, grad_up, grad_out_weight, grad_qkv)
    )
    grad_gain_one = butterfly(grad_gain_one, "tp", n_tp)
    gain_grads = jnp.stack([grad_gain_one, grad_gain_two])
    gain_grads = butterfly(butterfly(gain_grads, "fsdp", n_fsdp), "ctx", n_ctx)
    gain_grads = columns(gain_grads, fsdp)
    return (result, grad_tokens, gain_grads[0], grad_qkv, grad_out_weight, gain_grads[1], grad_up, grad_down)


def solution(mesh):
    return jax.shard_map(
        partial(shards, dict(mesh.shape)),
        mesh=mesh,
        in_specs=(
            P("fsdp", "ctx", None),
            P("fsdp", "ctx"),
            P("fsdp"),
            P(None, "fsdp", "tp"),
            P("tp", "fsdp"),
            P("fsdp"),
            P("fsdp", "tp"),
            P("tp", "fsdp"),
            P("fsdp", "ctx", None),
        ),
        out_specs=(
            P("fsdp", "ctx", None),
            P("fsdp", "ctx", None),
            P("fsdp"),
            P(None, "fsdp", "tp"),
            P("tp", "fsdp"),
            P("fsdp"),
            P("fsdp", "tp"),
            P("tp", "fsdp"),
        ),
        check_vma=False,
    )
```
